32 devices in a mesh: groups: 2 (over y), seq: 4 (over z), weight: 4 (over x, core).
Axes of the slice: x: 2, y: 2, z: 4, core: 2. Of those that a mesh axis runs over, the one named last changes fastest.
Arguments:
- tokens: bfloat16 [8, 512, 1536], P(('groups', 'weight'), 'seq'), parts along dimension 0, may hold values from -20 to 20
- upstream_grad: bfloat16 [8, 512, 1536], P(('groups', 'weight'), 'seq'), parts along dimension 0, may hold values from -6 to 6
- norm_gain: float32 [1536], replicated, may hold values from 0.5 to 1.5
- norm_bias: float32 [1536], replicated, may hold values from -3 to 3
- input_codes: bfloat16 [1536, 2304], P('weight'), may hold values from -10 to 10
- input_scales: float32 [12, 18], P('weight'), may hold values from 0.02 to 0.06
- input_bias: float32 [2304], replicated, may hold values from -3 to 3
- output_codes: bfloat16 [768, 1536], replicated, may hold values from -4 to 4
- output_scales: float32 [6, 12], replicated, may hold values from 0.02 to 0.06
- layer_scale: float32 [1536], replicated, may hold values from 0.3 to 3
Outputs:
- input_grad: float32 [8, 512, 1536], P(('groups', 'weight'), 'seq'), parts along dimension 0
The draws below stay inside these ranges and needn't reach their ends.
There are 2 independent parts, one for each index of `groups`. The reference program is written for one: setup_inputs(seed, part) draws one part's arguments, and reference() takes and returns one part's arrays. A program takes and returns all parts, laid end to end along the dimension named above; an argument that names none is the same for every part. Nothing has to cross between parts.
All inputs are finite; a program needn't handle non-finite values.
Results may differ from the reference program's by a relative error of at most 0.024.
Values may be sent and summed in bfloat16 or wider, within the bound.
A program may use at most 128 MiB of HBM per device.

```python
import math
import jax
import jax.numpy as jnp
from jax import lax

D = 1536
HEADS = 12
HEAD_DIM = 64
QBLOCK = 128
TOK_DEV = 128
HD = 768
SEQ = 512
IMAGES = 4
N_SEQ = 4


def draw_tokens(key, part):
    first_key = jax.random.fold_in(key, 0)
    sample = jax.random.normal(first_key, (IMAGES, SEQ, D), jnp.float32)
    return jnp.clip(sample, -6.0, 6.0).astype(jnp.bfloat16)


def draw_input_codes(key, part):
    first_key = jax.random.fold_in(key, 0)
    sample = jnp.clip(jax.random.normal(first_key, (D, 3 * HD), jnp.float32), -4.0, 4.0)
    return sample.astype(jnp.bfloat16)


def levels(stream_key, shape, cuts, low, high):
    loudness = 1.0
    for axis_at, blocks in cuts:
        steps = jax.random.uniform(jax.random.fold_in(jax.random.fold_in(stream_key, 6), axis_at), (blocks,), jnp.float32, low / len(cuts), high / len(cuts))
        loudness = loudness * jnp.repeat(jnp.exp(steps), shape[axis_at] // blocks).reshape((-1,) + (1,) * (len(shape) - 1 - axis_at))
    return loudness


def normal_values(stream_key, shape, scale, bound, shards=(), dtype=jnp.bfloat16):
    result = jax.random.normal(stream_key, shape, jnp.float32) * scale
    if len(shards) > 0:
        result = levels(stream_key, shape, shards, -0.22, 0.18) * result
    return jnp.clip(result, min=-bound, max=bound).astype(dtype)


def setup_inputs(seed: int = 0, part: int = 0) -> dict:
    keys = jax.random.split(jax.random.key(seed), 11)
    part_splits = jax.random.split(jax.random.fold_in(keys[10], part), 11)
    return {
        "tokens": draw_tokens(jax.random.fold_in(jax.random.fold_in(keys[10], part), 71), part),
        "upstream_grad": normal_values(part_splits[1], (IMAGES, SEQ, D), 1.0, 6.0, ((0, 4), (1, 4))),
        "norm_gain": jnp.clip(1.0 + 0.1 * jax.random.normal(keys[2], (D,), jnp.float32), 0.5, 1.5),
        "norm_bias": normal_values(keys[3], (D,), 0.5, 3.0, (), jnp.float32),
        "input_codes": draw_input_codes(jax.random.fold_in(keys[10], 71), part),
        "input_scales": jnp.clip(jnp.exp(math.log(0.06) - 1.0986123 * jax.random.uniform(keys[5], (D // QBLOCK, 3 * HD // QBLOCK), jnp.float32) ** levels(keys[5], (D // QBLOCK, 3 * HD // QBLOCK), ((0, 4),), -0.2, 0.2)), 0.02, 0.06),
        "input_bias": normal_values(keys[6], (3 * HD,), 0.5, 3.0, (), jnp.float32),
        "output_codes": normal_values(keys[7], (HD, D), 1.0, 4.0),
        "output_scales": jnp.clip(jnp.exp(jax.random.uniform(keys[8], (HD // QBLOCK, D // QBLOCK), jnp.float32, math.log(0.02), math.log(0.06))), 0.02, 0.06),
        "layer_scale": jnp.clip(jnp.exp(jax.random.uniform(keys[9], (D,), jnp.float32, math.log(0.3), math.log(3.0))), 0.3, 3.0),
    }


def dequantize(codes, scales):
    expanded = jnp.repeat(jnp.repeat(scales, QBLOCK, axis=0), QBLOCK, axis=1)
    return (codes.astype(jnp.float32) * expanded).astype(jnp.bfloat16)

def normalize(rows, gain, shift):
    mean_value = lax.optimization_barrier(jnp.mean(rows, axis=-1, keepdims=True))
    centered = rows - mean_value
    variance = lax.optimization_barrier(jnp.mean(centered * centered, axis=-1, keepdims=True))
    inverse = lax.rsqrt(variance + 1e-06)
    normed = centered * inverse
    return (normed, inverse, (normed * gain + shift).astype(jnp.bfloat16))

def norm_backward(grad_norm, normed, inverse, gain):
    grad_hat = grad_norm * gain
    first_mean = lax.optimization_barrier(jnp.mean(grad_hat, axis=-1, keepdims=True))
    second_mean = lax.optimization_barrier(jnp.mean(grad_hat * normed, axis=-1, keepdims=True))
    return inverse * (grad_hat - first_mean - normed * second_mean)

def rounded_total(terms):
    rounded = lax.optimization_barrier(terms.astype(jnp.bfloat16))
    return lax.optimization_barrier(jnp.sum(rounded.astype(jnp.float32), axis=0))

def head_backward(queries, keys_head, values_head, grads_head):
    head_scale = HEAD_DIM ** (-0.5)
    scores = jnp.dot(queries, keys_head.T, preferred_element_type=jnp.float32) * head_scale
    row_top = lax.optimization_barrier(jnp.max(scores, axis=1, keepdims=True))
    log_total = row_top + jnp.log(lax.optimization_barrier(jnp.sum(jnp.exp(scores - row_top), axis=1, keepdims=True)))
    dprob = jnp.dot(grads_head, values_head.T, preferred_element_type=jnp.float32)
    weights = jnp.exp(scores - log_total)
    row_delta = lax.optimization_barrier(jnp.sum(weights * dprob, axis=1, keepdims=True))
    prob_weights = weights.astype(jnp.bfloat16)
    dscore = (weights * (dprob - row_delta)).astype(jnp.bfloat16)
    query_grad = jnp.dot(dscore, keys_head, preferred_element_type=jnp.float32) * head_scale
    dscore_parts = dscore.astype(jnp.float32).reshape(N_SEQ, TOK_DEV, SEQ)
    prob_parts = prob_weights.astype(jnp.float32).reshape(N_SEQ, TOK_DEV, SEQ)
    query_parts = queries.astype(jnp.float32).reshape(N_SEQ, TOK_DEV, HEAD_DIM)
    grad_parts = grads_head.astype(jnp.float32).reshape(N_SEQ, TOK_DEV, HEAD_DIM)
    key_grad = rounded_total(jnp.einsum('sqk,sqd->skd', dscore_parts, query_parts) * head_scale)
    value_grad = rounded_total(jnp.einsum('sqk,sqd->skd', prob_parts, grad_parts))
    return (query_grad, key_grad, value_grad)

def split_heads(columns):
    return columns.reshape(SEQ, HEADS, HEAD_DIM).transpose(1, 0, 2)

def merge_heads(stacked):
    return stacked.transpose(1, 0, 2).reshape(SEQ, HD)

def reference(tokens, upstream_grad, norm_gain, norm_bias, input_codes, input_scales, input_bias, output_codes, output_scales, layer_scale):
    input_weight = dequantize(input_codes, input_scales)
    output_weight = dequantize(output_codes, output_scales)

    def one_image(packed):
        image_rows, image_grads = packed
        normed, inverse, norm_out = normalize(image_rows.astype(jnp.float32), norm_gain, norm_bias)
        projected = (jnp.dot(norm_out, input_weight, preferred_element_type=jnp.float32) + input_bias).astype(jnp.bfloat16)
        scaled_grad = (image_grads.astype(jnp.float32) * layer_scale).astype(jnp.bfloat16)
        head_grads = jnp.dot(scaled_grad, output_weight.T, preferred_element_type=jnp.float32).astype(jnp.bfloat16)
        heads_in = (split_heads(projected[:, :HD]), split_heads(projected[:, HD:2 * HD]), split_heads(projected[:, 2 * HD:]), split_heads(head_grads))
        query_grad, key_grad, value_grad = lax.map(lambda member: head_backward(*member), heads_in)
        grad_proj = jnp.concatenate([merge_heads(query_grad), merge_heads(key_grad), merge_heads(value_grad)], axis=1).astype(jnp.bfloat16)
        grad_norm = jnp.dot(grad_proj, input_weight.T, preferred_element_type=jnp.float32)
        return norm_backward(grad_norm, normed, inverse, norm_gain)
    return lax.map(one_image, (tokens, upstream_grad))
```

```python
import functools
import math

import jax
import jax.numpy as jnp
from jax import lax
from jax.experimental import pallas as pl
from jax.experimental.pallas import tpu as pltpu
from jax.sharding import PartitionSpec as P

HEADS = 12
HEAD_DIM = 64
QBLOCK = 128
HD = 768


def dequantize(codes, scales):
    expanded = jnp.repeat(jnp.repeat(scales, QBLOCK, axis=0), QBLOCK, axis=1)
    return (codes.astype(jnp.float32) * expanded).astype(jnp.bfloat16)


def normalize(rows, gain, shift):
    mean_value = jnp.mean(rows, axis=-1, keepdims=True)
    centered = rows - mean_value
    variance = jnp.mean(centered * centered, axis=-1, keepdims=True)
    inverse = lax.rsqrt(variance + 1e-06)
    normed = centered * inverse
    return (normed, inverse, (normed * gain + shift).astype(jnp.bfloat16))


def norm_backward(grad_norm, normed, inverse, gain):
    grad_hat = grad_norm * gain
    first_mean = jnp.mean(grad_hat, axis=-1, keepdims=True)
    second_mean = jnp.mean(grad_hat * normed, axis=-1, keepdims=True)
    return inverse * (grad_hat - first_mean - normed * second_mean)


def score_block(queries, head_grads, pair_block):
    row_count = pair_block.shape[0]
    keys_blk = pair_block[:, :HD].reshape(row_count, HEADS, HEAD_DIM)
    values_blk = pair_block[:, HD:].reshape(row_count, HEADS, HEAD_DIM)
    scores = jnp.einsum(
        "qhd,khd->hqk", queries, keys_blk, preferred_element_type=jnp.float32
    ) * HEAD_DIM ** (-0.5)
    dprob = jnp.einsum("qhd,khd->hqk", head_grads, values_blk, preferred_element_type=jnp.float32)
    return (keys_blk, scores, dprob)


def update_stats(statistics, queries, head_grads, pair_rows):
    sub_size = math.gcd(pair_rows.shape[0], 512)

    def visit_block(block_index, running):
        run_max, run_total, run_mix = running
        pair_block = lax.dynamic_slice_in_dim(pair_rows, block_index * sub_size, sub_size, 0)
        keys_blk, scores, dprob = score_block(queries, head_grads, pair_block)
        new_max = jnp.maximum(run_max, jnp.max(scores, axis=-1))
        factor = jnp.exp(run_max - new_max)
        expo = jnp.exp(scores - new_max[..., None])
        return (
            new_max,
            run_total * factor + jnp.sum(expo, axis=-1),
            run_mix * factor + jnp.sum(expo * dprob, axis=-1),
        )

    return lax.fori_loop(0, pair_rows.shape[0] // sub_size, visit_block, statistics)


def block_backward(queries, head_grads, pair_block, log_total, row_delta):
    keys_blk, scores, dprob = score_block(queries, head_grads, pair_block)
    weights = jnp.exp(scores - log_total[..., None])
    prob_weights = weights.astype(jnp.bfloat16)
    dscore = (weights * (dprob - row_delta[..., None])).astype(jnp.bfloat16)
    return (keys_blk, prob_weights, dscore)


def key_terms_from(queries, head_grads, prob_weights, dscore):
    key_part = jnp.einsum(
        "hqk,qhd->khd", dscore, queries, preferred_element_type=jnp.float32
    ) * HEAD_DIM ** (-0.5)
    value_part = jnp.einsum(
        "hqk,qhd->khd", prob_weights, head_grads, preferred_element_type=jnp.float32
    )
    row_count = key_part.shape[0]
    return jnp.concatenate(
        [key_part.reshape(row_count, HD), value_part.reshape(row_count, HD)], axis=1
    )


def query_side(queries, head_grads, keys_values, local_rows):
    seq_rows = local_rows * lax.axis_size("seq")
    start_stats = (
        jnp.full((HEADS, local_rows), -1e30, jnp.float32),
        jnp.zeros((HEADS, local_rows), jnp.float32),
        jnp.zeros((HEADS, local_rows), jnp.float32),
    )
    all_pairs = lax.all_gather(keys_values, "seq", axis=0, tiled=True)
    statistics = update_stats(start_stats, queries, head_grads, all_pairs)
    row_max, row_total, row_mix = statistics
    log_total = row_max + jnp.log(row_total)
    row_delta = row_mix / row_total
    sub_size = math.gcd(seq_rows, 512)
    block_count = seq_rows // sub_size
    empty_query = jnp.zeros((local_rows, HEADS, HEAD_DIM), jnp.float32)

    def backward_step(block_index, running):
        query_grad, buffer = running
        pair_block = lax.dynamic_slice_in_dim(all_pairs, block_index * sub_size, sub_size, 0)
        keys_blk, prob_weights, dscore = block_backward(
            queries, head_grads, pair_block, log_total, row_delta
        )
        query_grad = query_grad + jnp.einsum(
            "hqk,khd->qhd", dscore, keys_blk, preferred_element_type=jnp.float32
        )
        block_terms = key_terms_from(queries, head_grads, prob_weights, dscore)
        buffer = lax.dynamic_update_slice_in_dim(buffer, block_terms, block_index * sub_size, 0)
        return (query_grad, buffer)

    empty_terms = jnp.zeros((seq_rows, 2 * HD), jnp.float32)
    query_grad, buffer = lax.fori_loop(0, block_count, backward_step, (empty_query, empty_terms))
    pair_grads = lax.psum_scatter(
        buffer.astype(jnp.bfloat16), "seq", scatter_dimension=0, tiled=True
    ).astype(jnp.float32)
    return (query_grad, pair_grads)


def general(
    tokens,
    upstream_grad,
    norm_gain,
    norm_bias,
    input_codes,
    input_scales,
    input_bias,
    output_codes,
    output_scales,
    layer_scale,
):
    all_codes, all_scales = (
        lax.all_gather(input_codes.astype(jnp.float32), "weight", axis=0, tiled=True).astype(
            input_codes.dtype
        ),
        lax.all_gather(input_scales, "weight", axis=0, tiled=True),
    )
    input_weight = dequantize(all_codes, all_scales)
    output_weight = dequantize(output_codes, output_scales)
    normed, inverse, norm_out = normalize(tokens[0].astype(jnp.float32), norm_gain, norm_bias)
    projected = (
        jnp.dot(norm_out, input_weight, preferred_element_type=jnp.float32) + input_bias
    ).astype(jnp.bfloat16)
    local_rows = projected.shape[0]
    queries = projected[:, :HD].reshape(local_rows, HEADS, HEAD_DIM)
    keys_values = projected[:, HD:]
    scaled_grad = (upstream_grad[0].astype(jnp.float32) * layer_scale).astype(jnp.bfloat16)
    head_grads = jnp.dot(scaled_grad, output_weight.T, preferred_element_type=jnp.float32).astype(
        jnp.bfloat16
    )
    head_grads = head_grads.reshape(local_rows, HEADS, HEAD_DIM)
    query_grad, pair_grads = query_side(queries, head_grads, keys_values, local_rows)
    query_grad = (query_grad * HEAD_DIM ** (-0.5)).reshape(local_rows, HD)
    grad_proj = jnp.concatenate([query_grad, pair_grads], axis=1).astype(jnp.bfloat16)
    grad_norm = jnp.dot(grad_proj, input_weight.T, preferred_element_type=jnp.float32)
    result = norm_backward(grad_norm, normed, inverse, norm_gain)
    return result[None]


WIDTH = 1536
ROWS = 128
SHARD = 384
HALF = 384
GROUP = 192
BF16 = jnp.bfloat16
F32 = jnp.float32
MESH = pl.DeviceIdType.MESH
NT = (((1,), (1,)), ((), ()))


def fits(mesh):
    return dict(mesh.shape) == {"groups": 2, "seq": 4, "weight": 4}


def fused_kernel(
    tokens_hbm,
    upstream_hbm,
    gain_ref,
    norm_bias_ref,
    codes_hbm,
    in_scales,
    in_bias_ref,
    out_codes_hbm,
    out_scales,
    layer_scale_ref,
    out_ref,
    weight,
    codes,
    out_codes,
    out_weight,
    tokens,
    upstream,
    normed_buf,
    inverse_buf,
    norm_out,
    scaled,
    packed,
    gathered,
    grads,
    grad_proj,
    load_sem,
    w_send,
    w_recv,
    a_send,
    a_recv,
    g_send,
    g_recv,
):
    g = lax.axis_index("groups")
    s = lax.axis_index("seq")
    w = lax.axis_index("weight")
    core = lax.rem(w, 2)
    across = lax.rem(w + 2, 4)
    sibling = w + 1 - 2 * core
    far_sibling = lax.rem(sibling + 2, 4)
    near = s // 2
    far = 1 - near
    buddy = s + 1 - 2 * lax.rem(s, 2)
    parity = lax.rem(s, 2)

    def load(index, source, target):
        copy = pltpu.make_async_copy(source, target, load_sem.at[index])
        copy.start()
        return copy

    load_codes = load(0, codes_hbm, codes)
    load_tokens = load(1, tokens_hbm.at[0], tokens)
    load_upstream = load(2, upstream_hbm.at[0], upstream)
    load_out_codes = load(3, out_codes_hbm, out_codes)

    barrier = pltpu.get_barrier_semaphore()
    peers = [{"weight": across}, {"weight": sibling}, {"groups": 1 - g}]
    peers += [{"seq": lax.rem(s + k, 4)} for k in (1, 2, 3)]
    for peer in peers:
        pl.semaphore_signal(barrier, inc=1, device_id=peer, device_id_type=MESH)

    def half_of(j):
        return far if j < 3 else near

    def columns_of(j):
        return pl.ds(pl.multiple_of(768 * (j % 3) + HALF * half_of(j), 128), HALF)

    def dequantize_chunk(j):
        first = 6 * (j % 3) + 3 * half_of(j)
        for rb in range(3):
            for cb in range(3):
                cols = pl.ds(pl.multiple_of(128 * (first + cb), 128), 128)
                rows = pl.ds(pl.multiple_of(SHARD * w + 128 * rb, 128), 128)
                block = codes[128 * rb : 128 * (rb + 1), cols].astype(F32)
                weight[rows, cols] = (block * in_scales[rb, first + cb]).astype(BF16)

    def weight_copy(kind, j, row, count, peer):
        part = weight.at[pl.ds(pl.multiple_of(row, 64), count), columns_of(j)]
        return pltpu.make_async_remote_copy(
            src_ref=part,
            dst_ref=part,
            send_sem=w_send.at[kind, j],
            recv_sem=w_recv.at[kind, j],
            device_id=peer,
            device_id_type=MESH,
        )

    def x_copy(j, owner):
        return weight_copy(0, j, SHARD * owner + GROUP * g, GROUP, {"weight": across})

    def y_copy(j, part):
        return weight_copy(1, j, SHARD * across + GROUP * part, GROUP, {"groups": 1 - g})

    def own_copy(j, owner):
        return weight_copy(2, j, SHARD * owner, SHARD, {"weight": sibling})

    def passed_copy(j, owner):
        return weight_copy(3, j, SHARD * owner, SHARD, {"weight": sibling})

    def start_own(j):
        x_copy(j, w).start()
        own_copy(j, w).start()

    def exchange(t, dest, send_index, recv_index):
        return pltpu.make_async_remote_copy(
            src_ref=packed.at[t, pl.ds(pl.multiple_of(GROUP * dest, 64), GROUP), :],
            dst_ref=gathered.at[t, s],
            send_sem=a_send.at[t, send_index],
            recv_sem=a_recv.at[t, recv_index],
            device_id={"seq": dest},
            device_id_type=MESH,
        )

    def exchange_done(t, source, index):
        return pltpu.make_async_remote_copy(
            src_ref=packed.at[t, pl.ds(pl.multiple_of(GROUP * source, 64), GROUP), :],
            dst_ref=gathered.at[t, source],
            send_sem=a_send.at[t, index],
            recv_sem=a_recv.at[t, index],
            device_id={"seq": source},
            device_id_type=MESH,
        )

    def share(t, is_far, value):
        half = far if is_far else near
        packed[t, pl.ds(pl.multiple_of(HALF * half, 128), HALF), :] = value
        if is_far:
            for k in range(2):
                exchange(t, 2 * far + k, k, parity).start()
        else:
            exchange(t, buddy, 2, 2).start()
            gathered[t, s] = packed[t, pl.ds(pl.multiple_of(GROUP * s, 64), GROUP), :]

    def head_gradients(is_far):
        half = far if is_far else near
        for rb in range(3):
            rows = pl.ds(pl.multiple_of(HALF * half + 128 * rb, 128), 128)
            for cb in range(12):
                block = out_codes[rows, 128 * cb : 128 * (cb + 1)].astype(F32)
                out_weight[128 * rb : 128 * (rb + 1), 128 * cb : 128 * (cb + 1)] = (
                    block * out_scales[3 * half + rb, cb]
                ).astype(BF16)
        value = lax.dot_general(out_weight[...], scaled[...], NT, preferred_element_type=F32)
        share(3, is_far, value.astype(BF16))

    def project(j):
        value = jnp.dot(norm_out[...], weight[:, columns_of(j)], preferred_element_type=F32)
        value = value + in_bias_ref[:, columns_of(j)]
        if j % 3 == 0:
            value = value * HEAD_DIM ** (-0.5)
        share(j % 3, j < 3, value.T.astype(BF16))

    load_codes.wait()
    dequantize_chunk(0)
    dequantize_chunk(1)
    pl.semaphore_wait(barrier, 6)
    start_own(0)
    start_own(1)
    for j in range(2, 6):
        dequantize_chunk(j)

    load_upstream.wait()
    scaled[...] = (upstream[...].astype(F32) * layer_scale_ref[...]).astype(BF16)
    load_out_codes.wait()
    head_gradients(True)

    load_tokens.wait()
    normed, inverse, rounded = normalize(
        tokens[...].astype(F32), gain_ref[...], norm_bias_ref[...]
    )
    normed_buf[...] = normed
    inverse_buf[...] = inverse
    norm_out[...] = rounded

    for step in range(8):
        if step < 6:
            x_copy(step, across).wait_recv()
            if step + 2 < 6:
                start_own(step + 2)
            y_copy(step, g).start()
        if 1 <= step < 7:
            y_copy(step - 1, 1 - g).wait_recv()
            passed_copy(step - 1, across).start()
        if step == 0:
            head_gradients(False)
        if step >= 2:
            own_copy(step - 2, sibling).wait_recv()
            passed_copy(step - 2, far_sibling).wait_recv()
            project(step - 2)

    for t in (0, 1, 2, 3):
        for k in range(2):
            exchange_done(t, 2 * far + k, k).wait_recv()
        exchange_done(t, buddy, 2).wait_recv()

    def grad_copy(h, dest, source, send_index, recv_index, peer):
        rows = pl.ds(pl.multiple_of(GROUP * source + HEAD_DIM * h, 64), HEAD_DIM)
        return pltpu.make_async_remote_copy(
            src_ref=grads.at[h, dest],
            dst_ref=grad_proj.at[:, rows, :],
            send_sem=g_send.at[h, send_index],
            recv_sem=g_recv.at[h, recv_index],
            device_id={"seq": peer},
            device_id_type=MESH,
        )

    for h in range(3):
        rows = slice(HEAD_DIM * h, HEAD_DIM * (h + 1))
        q_t, k_t, v_t, g_t = (
            jnp.concatenate([gathered[t, i, rows, :] for i in range(4)], axis=1) for t in range(4)
        )
        scores = jnp.dot(k_t.T, q_t, preferred_element_type=F32)
        dprob = jnp.dot(v_t.T, g_t, preferred_element_type=F32)
        expo = jnp.exp(scores - jnp.max(scores, axis=0, keepdims=True))
        probs = expo * (1.0 / jnp.sum(expo, axis=0, keepdims=True))
        delta = jnp.sum(probs * dprob, axis=0, keepdims=True)
        dscore = (probs * (dprob - delta)).astype(BF16)
        parts = (
            jnp.dot(k_t, dscore, preferred_element_type=F32) * HEAD_DIM ** (-0.5),
            lax.dot_general(q_t, dscore, NT, preferred_element_type=F32),
            lax.dot_general(g_t, probs.astype(BF16), NT, preferred_element_type=F32),
        )
        for t in range(3):
            value = parts[t].astype(BF16)
            for i in range(4):
                grads[h, i, t] = value[:, ROWS * i : ROWS * (i + 1)]
        for k in range(2):
            grad_copy(h, 2 * far + k, s, k, parity, 2 * far + k).start()
        grad_copy(h, buddy, s, 2, 2, buddy).start()
        own = pl.ds(pl.multiple_of(GROUP * s + HEAD_DIM * h, 64), HEAD_DIM)
        grad_proj[:, own, :] = grads[h, s]

    def back(half):
        total = None
        for t in range(3):
            rows = pl.ds(pl.multiple_of(HALF * half, 128), HALF)
            cols = pl.ds(pl.multiple_of(768 * t + HALF * half, 128), HALF)
            term = lax.dot_general(
                grad_proj[t, rows, :].T, weight[:, cols], NT, preferred_element_type=F32
            )
            total = term if total is None else total + term
        return total

    for h in range(3):
        grad_copy(h, buddy, buddy, 2, 2, buddy).wait_recv()
    out_ref[0] = back(near)
    for h in range(3):
        for k in range(2):
            grad_copy(h, 2 * far + k, 2 * far + k, k, k, 2 * far + k).wait_recv()
    grad_norm = out_ref[0] + back(far)
    out_ref[0] = norm_backward(grad_norm, normed_buf[...], inverse_buf[...], gain_ref[...])

    for j in range(6):
        x_copy(j, w).wait_send()
        own_copy(j, w).wait_send()
        y_copy(j, g).wait_send()
        passed_copy(j, across).wait_send()
    for t in range(4):
        for k in range(2):
            exchange(t, 2 * far + k, k, parity).wait_send()
        exchange(t, buddy, 2, 2).wait_send()
    for h in range(3):
        for k in range(2):
            grad_copy(h, 2 * far + k, s, k, parity, 2 * far + k).wait_send()
        grad_copy(h, buddy, s, 2, 2, buddy).wait_send()


def fused(
    tokens,
    upstream_grad,
    norm_gain,
    norm_bias,
    input_codes,
    input_scales,
    input_bias,
    output_codes,
    output_scales,
    layer_scale,
):
    anywhere = pl.BlockSpec(memory_space=pl.ANY)
    vmem = pl.BlockSpec(memory_space=pltpu.VMEM)
    smem = pl.BlockSpec(memory_space=pltpu.SMEM)
    return pl.pallas_call(
        fused_kernel,
        out_shape=jax.ShapeDtypeStruct((1, ROWS, WIDTH), F32),
        in_specs=[anywhere, anywhere, vmem, vmem, anywhere, smem, vmem, anywhere, smem, vmem],
        out_specs=vmem,
        scratch_shapes=[
            pltpu.VMEM((WIDTH, 3 * HD), BF16),
            pltpu.VMEM((SHARD, 3 * HD), BF16),
            pltpu.VMEM((HD, WIDTH), BF16),
            pltpu.VMEM((HALF, WIDTH), BF16),
            pltpu.VMEM((ROWS, WIDTH), BF16),
            pltpu.VMEM((ROWS, WIDTH), BF16),
            pltpu.VMEM((ROWS, WIDTH), F32),
            pltpu.VMEM((ROWS, 1), F32),
            pltpu.VMEM((ROWS, WIDTH), BF16),
            pltpu.VMEM((ROWS, WIDTH), BF16),
            pltpu.VMEM((4, HD, ROWS), BF16),
            pltpu.VMEM((4, 4, GROUP, ROWS), BF16),
            pltpu.VMEM((3, 4, 3, HEAD_DIM, ROWS), BF16),
            pltpu.VMEM((3, HD, ROWS), BF16),
            pltpu.SemaphoreType.DMA((4,)),
            pltpu.SemaphoreType.DMA((4, 6)),
            pltpu.SemaphoreType.DMA((4, 6)),
            pltpu.SemaphoreType.DMA((4, 3)),
            pltpu.SemaphoreType.DMA((4, 3)),
            pltpu.SemaphoreType.DMA((3, 3)),
            pltpu.SemaphoreType.DMA((3, 3)),
        ],
        compiler_params=pltpu.CompilerParams(
            collective_id=0, has_side_effects=True, vmem_limit_bytes=52 * 1024 * 1024
        ),
        cost_estimate=pl.CostEstimate(
            flops=2500000000, bytes_accessed=8000000, transcendentals=1000000
        ),
    )(
        tokens,
        upstream_grad,
        norm_gain[None],
        norm_bias[None],
        input_codes,
        input_scales,
        input_bias[None],
        output_codes,
        output_scales,
        layer_scale[None],
    )


def solution(mesh):
    in_specs = (
        P(("groups", "weight"), "seq", None),
        P(("groups", "weight"), "seq", None),
        P(),
        P(),
        P("weight", None),
        P("weight", None),
        P(),
        P(),
        P(),
        P(),
    )
    out_specs = P(("groups", "weight"), "seq", None)
    local = fused if fits(mesh) else general
    return jax.shard_map(local, mesh=mesh, in_specs=in_specs, out_specs=out_specs, check_vma=False)
```

```python
import functools
import math

import jax
import jax.numpy as jnp
from jax import lax
from jax.experimental import pallas as pl
from jax.experimental.pallas import tpu as pltpu
from jax.sharding import PartitionSpec as P

HEADS = 12
HEAD_DIM = 64
QBLOCK = 128
HD = 768


def dequantize(codes, scales):
    expanded = jnp.repeat(jnp.repeat(scales, QBLOCK, axis=0), QBLOCK, axis=1)
    return (codes.astype(jnp.float32) * expanded).astype(jnp.bfloat16)


def normalize(rows, gain, shift):
    mean_value = jnp.mean(rows, axis=-1, keepdims=True)
    centered = rows - mean_value
    variance = jnp.mean(centered * centered, axis=-1, keepdims=True)
    inverse = lax.rsqrt(variance + 1e-06)
    normed = centered * inverse
    return (normed, inverse, (normed * gain + shift).astype(jnp.bfloat16))


def norm_backward(grad_norm, normed, inverse, gain):
    grad_hat = grad_norm * gain
    first_mean = jnp.mean(grad_hat, axis=-1, keepdims=True)
    second_mean = jnp.mean(grad_hat * normed, axis=-1, keepdims=True)
    return inverse * (grad_hat - first_mean - normed * second_mean)


def score_block(queries, head_grads, pair_block):
    row_count = pair_block.shape[0]
    keys_blk = pair_block[:, :HD].reshape(row_count, HEADS, HEAD_DIM)
    values_blk = pair_block[:, HD:].reshape(row_count, HEADS, HEAD_DIM)
    scores = jnp.einsum(
        "qhd,khd->hqk", queries, keys_blk, preferred_element_type=jnp.float32
    ) * HEAD_DIM ** (-0.5)
    dprob = jnp.einsum("qhd,khd->hqk", head_grads, values_blk, preferred_element_type=jnp.float32)
    return (keys_blk, scores, dprob)


def update_stats(statistics, queries, head_grads, pair_rows):
    sub_size = math.gcd(pair_rows.shape[0], 512)

    def visit_block(block_index, running):
        run_max, run_total, run_mix = running
        pair_block = lax.dynamic_slice_in_dim(pair_rows, block_index * sub_size, sub_size, 0)
        keys_blk, scores, dprob = score_block(queries, head_grads, pair_block)
        new_max = jnp.maximum(run_max, jnp.max(scores, axis=-1))
        factor = jnp.exp(run_max - new_max)
        expo = jnp.exp(scores - new_max[..., None])
        return (
            new_max,
            run_total * factor + jnp.sum(expo, axis=-1),
            run_mix * factor + jnp.sum(expo * dprob, axis=-1),
        )

    return lax.fori_loop(0, pair_rows.shape[0] // sub_size, visit_block, statistics)


def block_backward(queries, head_grads, pair_block, log_total, row_delta):
    keys_blk, scores, dprob = score_block(queries, head_grads, pair_block)
    weights = jnp.exp(scores - log_total[..., None])
    prob_weights = weights.astype(jnp.bfloat16)
    dscore = (weights * (dprob - row_delta[..., None])).astype(jnp.bfloat16)
    return (keys_blk, prob_weights, dscore)


def key_terms_from(queries, head_grads, prob_weights, dscore):
    key_part = jnp.einsum(
        "hqk,qhd->khd", dscore, queries, preferred_element_type=jnp.float32
    ) * HEAD_DIM ** (-0.5)
    value_part = jnp.einsum(
        "hqk,qhd->khd", prob_weights, head_grads, preferred_element_type=jnp.float32
    )
    row_count = key_part.shape[0]
    return jnp.concatenate(
        [key_part.reshape(row_count, HD), value_part.reshape(row_count, HD)], axis=1
    )


def query_side(queries, head_grads, keys_values, local_rows):
    seq_rows = local_rows * lax.axis_size("seq")
    start_stats = (
        jnp.full((HEADS, local_rows), -1e30, jnp.float32),
        jnp.zeros((HEADS, local_rows), jnp.float32),
        jnp.zeros((HEADS, local_rows), jnp.float32),
    )
    all_pairs = lax.all_gather(keys_values, "seq", axis=0, tiled=True)
    statistics = update_stats(start_stats, queries, head_grads, all_pairs)
    row_max, row_total, row_mix = statistics
    log_total = row_max + jnp.log(row_total)
    row_delta = row_mix / row_total
    sub_size = math.gcd(seq_rows, 512)
    block_count = seq_rows // sub_size
    empty_query = jnp.zeros((local_rows, HEADS, HEAD_DIM), jnp.float32)

    def backward_step(block_index, running):
        query_grad, buffer = running
        pair_block = lax.dynamic_slice_in_dim(all_pairs, block_index * sub_size, sub_size, 0)
        keys_blk, prob_weights, dscore = block_backward(
            queries, head_grads, pair_block, log_total, row_delta
        )
        query_grad = query_grad + jnp.einsum(
            "hqk,khd->qhd", dscore, keys_blk, preferred_element_type=jnp.float32
        )
        block_terms = key_terms_from(queries, head_grads, prob_weights, dscore)
        buffer = lax.dynamic_update_slice_in_dim(buffer, block_terms, block_index * sub_size, 0)
        return (query_grad, buffer)

    empty_terms = jnp.zeros((seq_rows, 2 * HD), jnp.float32)
    query_grad, buffer = lax.fori_loop(0, block_count, backward_step, (empty_query, empty_terms))
    pair_grads = lax.psum_scatter(
        buffer.astype(jnp.bfloat16), "seq", scatter_dimension=0, tiled=True
    ).astype(jnp.float32)
    return (query_grad, pair_grads)


def general(
    tokens,
    upstream_grad,
    norm_gain,
    norm_bias,
    input_codes,
    input_scales,
    input_bias,
    output_codes,
    output_scales,
    layer_scale,
):
    all_codes, all_scales = (
        lax.all_gather(input_codes.astype(jnp.float32), "weight", axis=0, tiled=True).astype(
            input_codes.dtype
        ),
        lax.all_gather(input_scales, "weight", axis=0, tiled=True),
    )
    input_weight = dequantize(all_codes, all_scales)
    output_weight = dequantize(output_codes, output_scales)
    normed, inverse, norm_out = normalize(tokens[0].astype(jnp.float32), norm_gain, norm_bias)
    projected = (
        jnp.dot(norm_out, input_weight, preferred_element_type=jnp.float32) + input_bias
    ).astype(jnp.bfloat16)
    local_rows = projected.shape[0]
    queries = projected[:, :HD].reshape(local_rows, HEADS, HEAD_DIM)
    keys_values = projected[:, HD:]
    scaled_grad = (upstream_grad[0].astype(jnp.float32) * layer_scale).astype(jnp.bfloat16)
    head_grads = jnp.dot(scaled_grad, output_weight.T, preferred_element_type=jnp.float32).astype(
        jnp.bfloat16
    )
    head_grads = head_grads.reshape(local_rows, HEADS, HEAD_DIM)
    query_grad, pair_grads = query_side(queries, head_grads, keys_values, local_rows)
    query_grad = (query_grad * HEAD_DIM ** (-0.5)).reshape(local_rows, HD)
    grad_proj = jnp.concatenate([query_grad, pair_grads], axis=1).astype(jnp.bfloat16)
    grad_norm = jnp.dot(grad_proj, input_weight.T, preferred_element_type=jnp.float32)
    result = norm_backward(grad_norm, normed, inverse, norm_gain)
    return result[None]


WIDTH = 1536
ROWS = 128
SHARD = 384
HALF = 384
GROUP = 192
BF16 = jnp.bfloat16
F32 = jnp.float32
MESH = pl.DeviceIdType.MESH
NT = (((1,), (1,)), ((), ()))


def fits(mesh):
    return dict(mesh.shape) == {"groups": 2, "seq": 4, "weight": 4}


def fused_kernel(
    tokens_hbm,
    upstream_hbm,
    gain_hbm,
    norm_bias_hbm,
    codes_hbm,
    in_scales_hbm,
    in_bias_hbm,
    out_codes_hbm,
    out_scales_hbm,
    layer_scale_hbm,
    out_ref,
    gain_ref,
    norm_bias_ref,
    in_scales,
    in_bias_ref,
    out_scales,
    layer_scale_ref,
    weight,
    codes,
    out_codes,
    out_weight,
    tokens,
    upstream,
    normed_buf,
    inverse_buf,
    norm_out,
    scaled,
    packed,
    gathered,
    grads,
    grad_proj,
    load_sem,
    w_send,
    w_recv,
    a_send,
    a_recv,
    g_send,
    g_recv,
):
    g = lax.axis_index("groups")
    s = lax.axis_index("seq")
    w = lax.axis_index("weight")
    core = lax.rem(w, 2)
    across = lax.rem(w + 2, 4)
    sibling = w + 1 - 2 * core
    far_sibling = lax.rem(sibling + 2, 4)
    near = s // 2
    far = 1 - near
    buddy = s + 1 - 2 * lax.rem(s, 2)
    parity = lax.rem(s, 2)

    def load(index, source, target):
        copy = pltpu.make_async_copy(source, target, load_sem.at[index])
        copy.start()
        return copy

    load_in_scales = load(4, in_scales_hbm, in_scales)
    load_codes = load(0, codes_hbm, codes)
    load_tokens = load(1, tokens_hbm.at[0], tokens)
    load_upstream = load(2, upstream_hbm.at[0], upstream)
    load_out_codes = load(3, out_codes_hbm, out_codes)
    load_out_scales = load(5, out_scales_hbm, out_scales)
    load_layer_scale = load(6, layer_scale_hbm, layer_scale_ref)
    load_gain = load(7, gain_hbm, gain_ref)
    load_norm_bias = load(8, norm_bias_hbm, norm_bias_ref)
    load_in_bias = load(9, in_bias_hbm, in_bias_ref)

    barrier = pltpu.get_barrier_semaphore()
    peers = [{"weight": across}, {"weight": sibling}, {"groups": 1 - g}]
    peers += [{"seq": lax.rem(s + k, 4)} for k in (1, 2, 3)]
    for peer in peers:
        pl.semaphore_signal(barrier, inc=1, device_id=peer, device_id_type=MESH)

    def half_of(j):
        return far if j < 3 else near

    def columns_of(j):
        return pl.ds(pl.multiple_of(768 * (j % 3) + HALF * half_of(j), 128), HALF)

    def dequantize_chunk(j):
        first = 6 * (j % 3) + 3 * half_of(j)
        for rb in range(3):
            for cb in range(3):
                cols = pl.ds(pl.multiple_of(128 * (first + cb), 128), 128)
                rows = pl.ds(pl.multiple_of(SHARD * w + 128 * rb, 128), 128)
                block = codes[128 * rb : 128 * (rb + 1), cols].astype(F32)
                weight[rows, cols] = (block * in_scales[rb, first + cb]).astype(BF16)

    def weight_copy(kind, j, row, count, peer):
        part = weight.at[pl.ds(pl.multiple_of(row, 64), count), columns_of(j)]
        return pltpu.make_async_remote_copy(
            src_ref=part,
            dst_ref=part,
            send_sem=w_send.at[kind, j],
            recv_sem=w_recv.at[kind, j],
            device_id=peer,
            device_id_type=MESH,
        )

    def x_copy(j, owner):
        return weight_copy(0, j, SHARD * owner + GROUP * g, GROUP, {"weight": across})

    def y_copy(j, part):
        return weight_copy(1, j, SHARD * across + GROUP * part, GROUP, {"groups": 1 - g})

    def own_copy(j, owner):
        return weight_copy(2, j, SHARD * owner, SHARD, {"weight": sibling})

    def passed_copy(j, owner):
        return weight_copy(3, j, SHARD * owner, SHARD, {"weight": sibling})

    def start_own(j):
        x_copy(j, w).start()
        own_copy(j, w).start()

    def exchange(t, dest, send_index, recv_index):
        return pltpu.make_async_remote_copy(
            src_ref=packed.at[t, pl.ds(pl.multiple_of(GROUP * dest, 64), GROUP), :],
            dst_ref=gathered.at[t, s],
            send_sem=a_send.at[t, send_index],
            recv_sem=a_recv.at[t, recv_index],
            device_id={"seq": dest},
            device_id_type=MESH,
        )

    def exchange_done(t, source, index):
        return pltpu.make_async_remote_copy(
            src_ref=packed.at[t, pl.ds(pl.multiple_of(GROUP * source, 64), GROUP), :],
            dst_ref=gathered.at[t, source],
            send_sem=a_send.at[t, index],
            recv_sem=a_recv.at[t, index],
            device_id={"seq": source},
            device_id_type=MESH,
        )

    def share(t, is_far, value):
        half = far if is_far else near
        packed[t, pl.ds(pl.multiple_of(HALF * half, 128), HALF), :] = value
        if is_far:
            for k in range(2):
                exchange(t, 2 * far + k, k, parity).start()
        else:
            exchange(t, buddy, 2, 2).start()
            gathered[t, s] = packed[t, pl.ds(pl.multiple_of(GROUP * s, 64), GROUP), :]

    def head_gradients(is_far):
        half = far if is_far else near
        for rb in range(3):
            rows = pl.ds(pl.multiple_of(HALF * half + 128 * rb, 128), 128)
            for cb in range(12):
                block = out_codes[rows, 128 * cb : 128 * (cb + 1)].astype(F32)
                out_weight[128 * rb : 128 * (rb + 1), 128 * cb : 128 * (cb + 1)] = (
                    block * out_scales[3 * half + rb, cb]
                ).astype(BF16)
        value = lax.dot_general(out_weight[...], scaled[...], NT, preferred_element_type=F32)
        share(3, is_far, value.astype(BF16))

    def project(j):
        value = jnp.dot(norm_out[...], weight[:, columns_of(j)], preferred_element_type=F32)
        value = value + in_bias_ref[columns_of(j)][None]
        if j % 3 == 0:
            value = value * HEAD_DIM ** (-0.5)
        share(j % 3, j < 3, value.T.astype(BF16))

    load_in_scales.wait()
    load_codes.wait()
    dequantize_chunk(0)
    dequantize_chunk(1)
    pl.semaphore_wait(barrier, 6)
    start_own(0)
    start_own(1)
    for j in range(2, 6):
        dequantize_chunk(j)

    load_layer_scale.wait()
    load_upstream.wait()
    scaled[...] = (upstream[...].astype(F32) * layer_scale_ref[...][None]).astype(BF16)
    load_out_scales.wait()
    load_out_codes.wait()
    head_gradients(True)

    load_gain.wait()
    load_norm_bias.wait()
    load_in_bias.wait()
    load_tokens.wait()
    normed, inverse, rounded = normalize(
        tokens[...].astype(F32), gain_ref[...][None], norm_bias_ref[...][None]
    )
    normed_buf[...] = normed
    inverse_buf[...] = inverse
    norm_out[...] = rounded

    for step in range(8):
        if step < 6:
            x_copy(step, across).wait_recv()
            if step + 2 < 6:
                start_own(step + 2)
            y_copy(step, g).start()
        if 1 <= step < 7:
            y_copy(step - 1, 1 - g).wait_recv()
            passed_copy(step - 1, across).start()
        if step == 0:
            head_gradients(False)
        if step >= 2:
            own_copy(step - 2, sibling).wait_recv()
            passed_copy(step - 2, far_sibling).wait_recv()
            project(step - 2)

    for t in (0, 1, 2, 3):
        for k in range(2):
            exchange_done(t, 2 * far + k, k).wait_recv()
        exchange_done(t, buddy, 2).wait_recv()

    def grad_copy(h, dest, source, send_index, recv_index, peer):
        rows = pl.ds(pl.multiple_of(GROUP * source + HEAD_DIM * h, 64), HEAD_DIM)
        return pltpu.make_async_remote_copy(
            src_ref=grads.at[h, dest],
            dst_ref=grad_proj.at[:, rows, :],
            send_sem=g_send.at[h, send_index],
            recv_sem=g_recv.at[h, recv_index],
            device_id={"seq": peer},
            device_id_type=MESH,
        )

    for h in range(3):
        rows = slice(HEAD_DIM * h, HEAD_DIM * (h + 1))
        q_t, k_t, v_t, g_t = (
            jnp.concatenate([gathered[t, i, rows, :] for i in range(4)], axis=1) for t in range(4)
        )
        scores = jnp.dot(k_t.T, q_t, preferred_element_type=F32)
        dprob = jnp.dot(v_t.T, g_t, preferred_element_type=F32)
        expo = jnp.exp(scores - jnp.max(scores, axis=0, keepdims=True))
        probs = expo * (1.0 / jnp.sum(expo, axis=0, keepdims=True))
        delta = jnp.sum(probs * dprob, axis=0, keepdims=True)
        dscore = (probs * (dprob - delta)).astype(BF16)
        parts = (
            jnp.dot(k_t, dscore, preferred_element_type=F32) * HEAD_DIM ** (-0.5),
            lax.dot_general(q_t, dscore, NT, preferred_element_type=F32),
            lax.dot_general(g_t, probs.astype(BF16), NT, preferred_element_type=F32),
        )
        for t in range(3):
            value = parts[t].astype(BF16)
            for i in range(4):
                grads[h, i, t] = value[:, ROWS * i : ROWS * (i + 1)]
        for k in range(2):
            grad_copy(h, 2 * far + k, s, k, parity, 2 * far + k).start()
        grad_copy(h, buddy, s, 2, 2, buddy).start()
        own = pl.ds(pl.multiple_of(GROUP * s + HEAD_DIM * h, 64), HEAD_DIM)
        grad_proj[:, own, :] = grads[h, s]

    def back(half):
        total = None
        for t in range(3):
            rows = pl.ds(pl.multiple_of(HALF * half, 128), HALF)
            cols = pl.ds(pl.multiple_of(768 * t + HALF * half, 128), HALF)
            term = lax.dot_general(
                grad_proj[t, rows, :].T, weight[:, cols], NT, preferred_element_type=F32
            )
            total = term if total is None else total + term
        return total

    for h in range(3):
        grad_copy(h, buddy, buddy, 2, 2, buddy).wait_recv()
    out_ref[0] = back(near)
    for h in range(3):
        for k in range(2):
            grad_copy(h, 2 * far + k, 2 * far + k, k, k, 2 * far + k).wait_recv()
    grad_norm = out_ref[0] + back(far)
    out_ref[0] = norm_backward(grad_norm, normed_buf[...], inverse_buf[...], gain_ref[...][None])

    for j in range(6):
        x_copy(j, w).wait_send()
        own_copy(j, w).wait_send()
        y_copy(j, g).wait_send()
        passed_copy(j, across).wait_send()
    for t in range(4):
        for k in range(2):
            exchange(t, 2 * far + k, k, parity).wait_send()
        exchange(t, buddy, 2, 2).wait_send()
    for h in range(3):
        for k in range(2):
            grad_copy(h, 2 * far + k, s, k, parity, 2 * far + k).wait_send()
        grad_copy(h, buddy, s, 2, 2, buddy).wait_send()


def fused(
    tokens,
    upstream_grad,
    norm_gain,
    norm_bias,
    input_codes,
    input_scales,
    input_bias,
    output_codes,
    output_scales,
    layer_scale,
):
    hbm = pl.BlockSpec(memory_space=pltpu.HBM)
    vmem = pl.BlockSpec(memory_space=pltpu.VMEM)
    return pl.pallas_call(
        fused_kernel,
        out_shape=jax.ShapeDtypeStruct((1, ROWS, WIDTH), F32),
        in_specs=[hbm] * 10,
        out_specs=vmem,
        scratch_shapes=[
            pltpu.VMEM((WIDTH,), F32),
            pltpu.VMEM((WIDTH,), F32),
            pltpu.SMEM((3, 18), F32),
            pltpu.VMEM((3 * HD,), F32),
            pltpu.SMEM((6, 12), F32),
            pltpu.VMEM((WIDTH,), F32),
            pltpu.VMEM((WIDTH, 3 * HD), BF16),
            pltpu.VMEM((SHARD, 3 * HD), BF16),
            pltpu.VMEM((HD, WIDTH), BF16),
            pltpu.VMEM((HALF, WIDTH), BF16),
            pltpu.VMEM((ROWS, WIDTH), BF16),
            pltpu.VMEM((ROWS, WIDTH), BF16),
            pltpu.VMEM((ROWS, WIDTH), F32),
            pltpu.VMEM((ROWS, 1), F32),
            pltpu.VMEM((ROWS, WIDTH), BF16),
            pltpu.VMEM((ROWS, WIDTH), BF16),
            pltpu.VMEM((4, HD, ROWS), BF16),
            pltpu.VMEM((4, 4, GROUP, ROWS), BF16),
            pltpu.VMEM((3, 4, 3, HEAD_DIM, ROWS), BF16),
            pltpu.VMEM((3, HD, ROWS), BF16),
            pltpu.SemaphoreType.DMA((10,)),
            pltpu.SemaphoreType.DMA((4, 6)),
            pltpu.SemaphoreType.DMA((4, 6)),
            pltpu.SemaphoreType.DMA((4, 3)),
            pltpu.SemaphoreType.DMA((4, 3)),
            pltpu.SemaphoreType.DMA((3, 3)),
            pltpu.SemaphoreType.DMA((3, 3)),
        ],
        compiler_params=pltpu.CompilerParams(
            collective_id=0, has_side_effects=True, vmem_limit_bytes=64 * 1024 * 1024 - 65536
        ),
        cost_estimate=pl.CostEstimate(
            flops=2500000000, bytes_accessed=8000000, transcendentals=1000000
        ),
    )(
        tokens,
        upstream_grad,
        norm_gain,
        norm_bias,
        input_codes,
        input_scales,
        input_bias,
        output_codes,
        output_scales,
        layer_scale,
    )


def solution(mesh):
    in_specs = (
        P(("groups", "weight"), "seq", None),
        P(("groups", "weight"), "seq", None),
        P(),
        P(),
        P("weight", None),
        P("weight", None),
        P(),
        P(),
        P(),
        P(),
    )
    out_specs = P(("groups", "weight"), "seq", None)
    local = fused if fits(mesh) else general
    return jax.shard_map(local, mesh=mesh, in_specs=in_specs, out_specs=out_specs, check_vma=False)
```
